256 devices in a mesh: gx: 32 (over x, z), gy: 8 (over y, core).
Axes of the slice: x: 4, y: 4, z: 8, core: 2. Of those that a mesh axis runs over, the one named last changes fastest.
Arguments:
- fields: float32 [5, 3, 4096, 4096], P(None, None, 'gx', 'gy'), may hold values from -6 to 6
- metric_first: float32 [4096], P('gx'), may hold values from 0.5 to 2
- metric_second: float32 [4096], P('gy'), may hold values from 0.5 to 2
Outputs:
- slope_first: float32 [5, 3, 4096, 4096], P(None, None, 'gx', 'gy')
- slope_second: float32 [5, 3, 4096, 4096], P(None, None, 'gx', 'gy')
The draws below stay inside these ranges and needn't reach their ends.
All inputs are finite; a program needn't handle non-finite values.
Results may differ from the reference program's by a relative error of at most 0.00007.
Values sent between devices are 32-bit elements; how exact they have to be, the bound alone decides.
No kernel may reach another device: no remote copies, remote signals or barrier semaphores. Data moves between devices by JAX's collectives and lax.ppermute only.
A program may use at most 128 MiB of HBM per device.

```python
import math
import jax
import jax.numpy as jnp
from jax import lax

FIELDS = 5
PLANES = 3
NX = 4096
NY = 4096


def block_levels(key, shape, pieces, low, high):
    def one(axis_at, parts):
        draws = jax.random.uniform(jax.random.fold_in(jax.random.fold_in(key, 6), axis_at), (parts,), jnp.float32, low / len(pieces), high / len(pieces))
        return jnp.repeat(jnp.exp(draws), shape[axis_at] // parts).reshape((-1,) + (1,) * (len(shape) - axis_at - 1))

    factor_of = one(*pieces[0])
    for cut in pieces[1:]:
        factor_of = factor_of * one(*cut)
    return factor_of


def normal_values(own_key, shape, scale, most, pieces=(), held_as=jnp.bfloat16):
    gain = block_levels(own_key, shape, pieces, -0.22, 0.18) if pieces else 1.0
    values = jax.random.normal(own_key, shape, jnp.float32) * scale * gain
    return jnp.minimum(jnp.maximum(values, -most), most).astype(held_as)


def setup_inputs(seed: int = 0) -> dict:
    arg_keys = jax.random.split(jax.random.key(seed), 4)
    fields = normal_values(arg_keys[0], (FIELDS, PLANES, NX, NY), 1.0, 6.0, ((2, 32), (3, 8)), jnp.float32)
    metric_first = jnp.clip(jnp.exp(math.log(2.0) - 1.3862944 * jax.random.uniform(arg_keys[1], (NX,), jnp.float32) ** block_levels(arg_keys[1], (NX,), ((0, 32),), -0.2, 0.2)), 0.5, 2.0)
    metric_second = jnp.clip(jnp.exp(math.log(2.0) - 1.3862944 * jax.random.uniform(arg_keys[2], (NY,), jnp.float32) ** block_levels(arg_keys[2], (NY,), ((0, 8),), -0.2, 0.2)), 0.5, 2.0)
    return dict(fields=fields, metric_first=metric_first, metric_second=metric_second)


ALPHA = 0.47
COEF_A = 2.0 * (ALPHA + 2.0) / 3.0
COEF_B = (4.0 * ALPHA - 1.0) / 3.0


def explicit_side(values, axis):
    return (COEF_A / 2.0) * (jnp.roll(values, -1, axis) - jnp.roll(values, 1, axis)) + (COEF_B / 4.0) * (jnp.roll(values, -2, axis) - jnp.roll(values, 2, axis))


def periodic_solve(forcing, axis):
    length = forcing.shape[axis]
    wave = jnp.arange(length, dtype=jnp.float32) * (2.0 * jnp.pi / length)
    symbol = 1.0 + 2.0 * ALPHA * jnp.cos(wave)
    profile = [1] * forcing.ndim
    profile[axis] = length
    spectrum = jnp.fft.fft(forcing, axis=axis) / symbol.reshape(profile)
    return jnp.real(jnp.fft.ifft(spectrum, axis=axis)).astype(forcing.dtype)


def reference(fields, metric_first, metric_second):
    def per_field(single):
        compact_first = periodic_solve(explicit_side(single, 1), 1)
        compact_second = periodic_solve(explicit_side(single, 2), 2)
        return compact_first * metric_first[None, :, None], compact_second * metric_second[None, None, :]

    slope_first, slope_second = lax.map(per_field, fields)
    return slope_first, slope_second
```

```python
import functools
import math
import numpy as np
import jax
import jax.numpy as jnp
from jax import lax
from jax.experimental import pallas as pl
from jax.experimental.pallas import tpu as pltpu
from jax.sharding import PartitionSpec as P

ALPHA = 0.47
STENCIL_NEAR = (ALPHA + 2.0) / 3.0
STENCIL_FAR = (4.0 * ALPHA - 1.0) / 12.0
ROOT = (math.sqrt(1.0 - 4.0 * ALPHA * ALPHA) - 1.0) / (2.0 * ALPHA)
PEAK = 1.0 / math.sqrt(1.0 - 4.0 * ALPHA * ALPHA)
DECAY = PEAK * (STENCIL_NEAR * (ROOT - 1.0 / ROOT) + STENCIL_FAR * (ROOT**2 - ROOT**-2))
NEXT = PEAK * STENCIL_FAR * (1.0 / ROOT - ROOT)
VMEM = 48 * 1024 * 1024


def kernel_matrix(extent):
    gap = np.arange(extent)[:, None] - np.arange(extent)[None, :]
    size = np.abs(gap)
    value = DECAY * ROOT ** size.astype(np.float64) + NEXT * (size == 1)
    return np.sign(gap) * value


def border_columns(extent):
    place = np.arange(extent)
    left = DECAY * ROOT ** place.astype(np.float64)
    return np.stack([left, -left[::-1], NEXT * (place == 0), -NEXT * (place == extent - 1)])


def split(value):
    high = value.astype(jnp.bfloat16)
    return high, (value - high.astype(jnp.float32)).astype(jnp.bfloat16)


def dot(left, right):
    return jnp.dot(left, right, preferred_element_type=jnp.float32)


def stacked(rows):
    high = rows.astype(jnp.bfloat16).astype(jnp.float32)
    low = (rows - high).astype(jnp.bfloat16).astype(jnp.float32)
    return jnp.concatenate([high, low, high, jnp.zeros_like(high)], axis=0).astype(jnp.bfloat16)


def moments_kernel(step, place_ref, u_ref, wx_ref, wy_ref, mx_ref, ox_ref, my_ref, oy_ref):
    g = pl.program_id(0)
    px = place_ref[0]
    py = place_ref[1]
    extent, width = u_ref.shape[1:]
    for t in range(step):
        f = g * step + t
        u = u_ref[t]
        right = jnp.zeros((8, width), jnp.float32)
        left = jnp.zeros((8, width), jnp.float32)
        for i in range(0, extent, 8):
            rows = u_ref[t, i : i + 8]
            right = right + rows * wx_ref[0, i : i + 8]
            left = left + rows * wx_ref[1, i : i + 8]
        mx_ref[0, pl.ds(f, 1), :] = jnp.sum(right, axis=0, keepdims=True)
        mx_ref[1, pl.ds(f, 1), :] = jnp.sum(left, axis=0, keepdims=True)
        head = u_ref[t, 0:1]
        tail = u_ref[t, extent - 1 : extent]
        mx_ref[2, pl.ds(f, 1), :] = jnp.where(px == 0, tail, head)
        ox_ref[pl.ds(f, 1), :] = jnp.where(px == 0, head, tail)
        half = width // 2
        turned = [u[:, c : c + 128].T for c in range(0, width, 128)]
        sums = []
        for side in range(2):
            for part in range(2):
                total = jnp.zeros((8, extent), jnp.float32)
                for j in range(part * half, (part + 1) * half, 8):
                    total = total + turned[j // 128][j % 128 : j % 128 + 8] * wy_ref[side, j - part * half : j - part * half + 8]
                sums.append(jnp.sum(total, axis=0, keepdims=True))
        low, high = turned[0][0:1], turned[-1][127:128]
        whole = ROOT**half
        my_ref[0, pl.ds(f, 1), :] = sums[1] + whole * sums[0]
        my_ref[1, pl.ds(f, 1), :] = sums[2] + whole * sums[3]
        my_ref[2, pl.ds(f, 1), :] = jnp.where(py == 0, high, low)
        oy_ref[0, pl.ds(f, 1), :] = jnp.where(py == 0, low, high)
        oy_ref[1, pl.ds(f, 1), :] = sums[0]
        oy_ref[2, pl.ds(f, 1), :] = sums[3]
        oy_ref[3, pl.ds(f, 1), :] = turned[half // 128 - 1][127:128]
        oy_ref[4, pl.ds(f, 1), :] = turned[half // 128][0:1]


def moments(place, cells, step=5):
    count, extent, width = cells.shape
    power = ROOT ** np.arange(1, extent + 1, dtype=np.float64)
    wx = np.broadcast_to(np.stack([power[::-1], power])[:, :, None], (2, extent, width)).astype(np.float32)
    power = ROOT ** np.arange(1, width // 2 + 1, dtype=np.float64)
    wy = np.broadcast_to(np.stack([power[::-1], power])[:, :, None], (2, width // 2, extent)).astype(np.float32)
    whole = lambda *shape: pl.BlockSpec(shape, lambda g: (0,) * len(shape))
    out = lambda *shape: jax.ShapeDtypeStruct(shape, jnp.float32)
    return pl.pallas_call(
        functools.partial(moments_kernel, step),
        grid=(count // step,),
        in_specs=[
            pl.BlockSpec(memory_space=pltpu.SMEM),
            pl.BlockSpec((step, extent, width), lambda g: (g, 0, 0)),
            whole(2, extent, width),
            whole(2, width // 2, extent),
        ],
        out_specs=[whole(3, count, width), whole(count, width), whole(3, count, extent), whole(5, count, extent)],
        out_shape=[out(3, count, width), out(count, width), out(3, count, extent), out(5, count, extent)],
        compiler_params=pltpu.CompilerParams(vmem_limit_bytes=VMEM),
        name="moments",
    )(place, cells, jnp.asarray(wx), jnp.asarray(wy))


def first_kernel(step, u_ref, v_ref, metric_ref, h_ref, c_ref, out_ref, one_ref, two_ref):
    g = pl.program_id(0)
    extent = u_ref.shape[1]

    @pl.when(g == 0)
    def _():
        row = lax.broadcasted_iota(jnp.int32, (extent, extent), 0)
        column = lax.broadcasted_iota(jnp.int32, (extent, extent), 1)
        metric = jnp.sum(jnp.where(row == column, metric_ref[...], 0.0), axis=1, keepdims=True)
        high, low = split(h_ref[...] * metric)
        one_ref[:, :extent] = high
        one_ref[:, extent:] = high
        two_ref[:, :extent] = low
        scaled = c_ref[...] * metric
        c_high = scaled.astype(jnp.bfloat16)
        c_low = (scaled - c_high.astype(jnp.float32)).astype(jnp.bfloat16)
        lane = lax.broadcasted_iota(jnp.int32, scaled.shape, 1)
        two_ref[:, extent:] = jnp.where(lane < 16, c_high.astype(jnp.float32), c_low.astype(jnp.float32)).astype(jnp.bfloat16)

    for t in range(step):
        f = g * step + t
        high, low = split(u_ref[t])
        rows = jnp.concatenate([v_ref[k, pl.ds(f, 1), :] for k in range(4)] + [jnp.zeros((4, u_ref.shape[2]), jnp.float32)], axis=0)
        total = dot(one_ref[...], jnp.concatenate([high, low], axis=0))
        total = total + dot(two_ref[...], jnp.concatenate([high, stacked(rows)], axis=0))
        out_ref[t] = total


def first(cells, border, metric, step=5):
    count, extent, width = cells.shape
    h = kernel_matrix(extent).astype(np.float32)
    c = np.zeros((extent, 32), np.float64)
    columns = border_columns(extent)
    for k in range(3):
        c[:, 8 * k : 8 * k + 4] = columns.T
    whole = lambda *shape: pl.BlockSpec(shape, lambda g: (0,) * len(shape))
    return pl.pallas_call(
        functools.partial(first_kernel, step),
        grid=(count // step,),
        in_specs=[
            pl.BlockSpec((step, extent, width), lambda g: (g, 0, 0)),
            whole(4, count, width),
            whole(1, extent),
            whole(extent, extent),
            whole(extent, 32),
        ],
        out_specs=pl.BlockSpec((step, extent, width), lambda g: (g, 0, 0)),
        out_shape=jax.ShapeDtypeStruct(cells.shape, jnp.float32),
        scratch_shapes=[pltpu.VMEM((extent, 2 * extent), jnp.bfloat16), pltpu.VMEM((extent, extent + 32), jnp.bfloat16)],
        compiler_params=pltpu.CompilerParams(vmem_limit_bytes=VMEM),
        name="slope_first",
    )(cells, border, metric.reshape(1, extent), jnp.asarray(h), jnp.asarray(c.astype(np.float32)))


def second_kernel(step, u_ref, v_ref, metric_ref, h_ref, c_ref, out_ref):
    g = pl.program_id(0)
    extent, width = u_ref.shape[1:]
    half = width // 2
    metric = metric_ref[...]
    for t in range(step):
        f = g * step + t
        rows = stacked(jnp.concatenate([v_ref[k, pl.ds(f, 1), :] for k in range(8)], axis=0))
        for part in range(2):
            at = slice(part * half, (part + 1) * half)
            high, low = split(u_ref[t, :, at])
            total = dot(high, h_ref[0]) + dot(low, h_ref[0]) + dot(high, h_ref[1])
            total = total + lax.dot_general(rows, c_ref[:, at], (((0,), (0,)), ((), ())), preferred_element_type=jnp.float32)
            out_ref[t, :, at] = total * metric[:, at]


def second(cells, border, metric, step=5):
    count, extent, width = cells.shape
    half = width // 2
    def halves(value):
        high = value.astype(np.float32).astype(jnp.bfloat16)
        return high, (value - high.astype(np.float64)).astype(np.float32).astype(jnp.bfloat16)
    h = np.stack(halves(kernel_matrix(half).T))
    c = np.zeros((8, width), np.float64)
    c[:4, :half] = border_columns(half)
    c[4:, half:] = border_columns(half)
    high, low = halves(c)
    c = np.concatenate([high, high, low, np.zeros_like(high)])
    whole = lambda *shape: pl.BlockSpec(shape, lambda g: (0,) * len(shape))
    return pl.pallas_call(
        functools.partial(second_kernel, step),
        grid=(count // step,),
        in_specs=[
            pl.BlockSpec((step, extent, width), lambda g: (g, 0, 0)),
            whole(8, count, extent),
            whole(1, width),
            whole(2, half, half),
            whole(32, width),
        ],
        out_specs=pl.BlockSpec((step, extent, width), lambda g: (g, 0, 0)),
        out_shape=jax.ShapeDtypeStruct(cells.shape, jnp.float32),
        compiler_params=pltpu.CompilerParams(vmem_limit_bytes=VMEM),
        name="slope_second",
    )(cells, border, metric.reshape(1, width), jnp.asarray(h), jnp.asarray(c))


def scan_table(devices, extent):
    levels = devices.bit_length() - 1
    table = np.zeros((devices, 6 * levels + 2), np.float64)
    ratio = ROOT**extent
    for d in range(devices):
        for k in range(levels):
            size = 1 << k
            weight = ratio**size
            upper = d >> k & 1
            place = d % size
            table[d, 6 * k : 6 * k + 6] = (
                (1.0, weight, weight, 1.0, ratio**place, 0.0)
                if upper
                else (weight, 1.0, 1.0, weight, 0.0, ratio ** (size - 1 - place))
            )
        table[d, -2:] = np.array([ratio**d, ratio ** (devices - 1 - d)]) / (1.0 - ratio**devices)
    return table.astype(np.float32)


def swap(block, axis, mask):
    return lax.ppermute(block, axis, [(i, i ^ mask) for i in range(lax.axis_size(axis))])


def swap_odd(block, axis):
    count = lax.axis_size(axis)
    return lax.ppermute(block, axis, [(i, (i + (1 if i % 2 else -1)) % count) for i in range(count)])


def gathered(message, spare, axis, extent, masks):
    count = lax.axis_size(axis)
    index = lax.axis_index(axis)
    row = lax.dynamic_index_in_dim(jnp.asarray(scan_table(count, extent)), index, keepdims=False)
    pair = lambda k: row[k : k + 2][:, None, None]
    other_edge = swap_odd(spare, axis)
    total = message[:2]
    outside = None
    for k, mask in enumerate(masks):
        reply = swap(message if k == 0 else total, axis, mask)
        if k == 0:
            edge = reply[2]
        term = pair(6 * k + 4) * reply[:2]
        outside = term if outside is None else outside + term
        total = pair(6 * k) * total + pair(6 * k + 2) * reply[:2]
    outside = outside + pair(6 * len(masks)) * total
    even = index % 2 == 0
    edges = jnp.stack([jnp.where(even, other_edge, edge), jnp.where(even, edge, other_edge)])
    return outside, edges


def shards(fields, metric_first, metric_second):
    fields_count, planes, extent, width = fields.shape
    cells = fields.reshape(fields_count * planes, extent, width)
    place = jnp.stack([lax.axis_index("gx") % 2, lax.axis_index("gy") % 2]).astype(jnp.int32)
    message_x, spare_x, message_y, own_y = moments(place, cells)
    outside_y, edges_y = gathered(message_y, own_y[0], "gy", width, (1, 2, 6))
    outside_x, edges_x = gathered(message_x, spare_x, "gx", extent, (1, 2, 7, 8, 24))
    ratio = ROOT ** (width // 2)
    border_y = jnp.stack(
        [
            outside_y[0],
            own_y[2] + ratio * outside_y[1],
            edges_y[0],
            own_y[4],
            own_y[1] + ratio * outside_y[0],
            outside_y[1],
            own_y[3],
            edges_y[1],
        ]
    )
    slope_second = second(cells, border_y, metric_second)
    slope_first = first(cells, jnp.concatenate([outside_x, edges_x]), metric_first)
    return slope_first.reshape(fields.shape), slope_second.reshape(fields.shape)


def solution(mesh):
    return jax.shard_map(
        shards,
        mesh=mesh,
        in_specs=(P(None, None, "gx", "gy"), P("gx"), P("gy")),
        out_specs=(P(None, None, "gx", "gy"), P(None, None, "gx", "gy")),
        check_vma=False,
    )
```

```python
import functools
import math
import numpy as np
import jax
import jax.numpy as jnp
from jax import lax
from jax.experimental import pallas as pl
from jax.experimental.pallas import tpu as pltpu
from jax.sharding import PartitionSpec as P

ALPHA = 0.47
STENCIL_NEAR = (ALPHA + 2.0) / 3.0
STENCIL_FAR = (4.0 * ALPHA - 1.0) / 12.0
ROOT = (math.sqrt(1.0 - 4.0 * ALPHA * ALPHA) - 1.0) / (2.0 * ALPHA)
PEAK = 1.0 / math.sqrt(1.0 - 4.0 * ALPHA * ALPHA)
DECAY = PEAK * (STENCIL_NEAR * (ROOT - 1.0 / ROOT) + STENCIL_FAR * (ROOT**2 - ROOT**-2))
NEXT = PEAK * STENCIL_FAR * (1.0 / ROOT - ROOT)
MASKS_X = ((1, 2, 3), (7,), (8, 16, 24))
MASKS_Y = ((1,), (3,), (7,))
VMEM = 16 * 1024 * 1024
VMEM_FULL = 50 * 1024 * 1024
VMEM_SECOND = 16 * 1024 * 1024
COST_SMALL = pl.CostEstimate(flops=8_000_000, bytes_accessed=8_000_000, transcendentals=0)
COST_FIRST = pl.CostEstimate(flops=3_000_000_000, bytes_accessed=8_000_000, transcendentals=0)
COST_SECOND = pl.CostEstimate(flops=300_000_000, bytes_accessed=8_000_000, transcendentals=0)


def kernel_matrix(extent):
    gap = np.arange(extent)[:, None] - np.arange(extent)[None, :]
    size = np.abs(gap)
    value = DECAY * ROOT ** size.astype(np.float64) + NEXT * (size == 1)
    return np.sign(gap) * value


def border_columns(extent):
    place = np.arange(extent)
    left = DECAY * ROOT ** place.astype(np.float64)
    return np.stack([left, -left[::-1], NEXT * (place == 0), -NEXT * (place == extent - 1)])


def split(value):
    high = value.astype(jnp.bfloat16)
    return high, (value - high.astype(jnp.float32)).astype(jnp.bfloat16)


def dot(left, right):
    return jnp.dot(left, right, preferred_element_type=jnp.float32)


def stacked(rows):
    high = rows.astype(jnp.bfloat16).astype(jnp.float32)
    low = (rows - high).astype(jnp.bfloat16).astype(jnp.float32)
    return jnp.concatenate([high, low, high, jnp.zeros_like(high)], axis=0).astype(jnp.bfloat16)


def row_weights(rows):
    place = lax.broadcasted_iota(jnp.int32, (8, 128), 0)
    down = jnp.zeros((8, 128), jnp.float32)
    up = jnp.zeros((8, 128), jnp.float32)
    for s in range(8):
        down = jnp.where(place == s, ROOT ** (8 - s), down)
        up = jnp.where(place == s, ROOT ** (s + 1), up)
    return down, up


def weighted_sums(load, extent):
    down, up = row_weights(8)
    right = left = None
    for i in range(0, extent, 8):
        rows = load(i)
        right = rows if right is None else right * ROOT**8 + rows
        rows = load(extent - 8 - i)
        left = rows if left is None else left * ROOT**8 + rows
    return jnp.sum(right * down, axis=0, keepdims=True), jnp.sum(left * up, axis=0, keepdims=True)


def first_moments_kernel(u_ref, kept_ref, mx_ref, total_ref, ox_ref, sems):
    even = lax.axis_index("gx") % 2 == 0
    count, extent, width = u_ref.shape
    copies = [pltpu.make_async_copy(u_ref.at[f], kept_ref.at[f], sems.at[f]) for f in range(count)]
    for copy in copies:
        copy.start()
    for f in range(count):
        copies[f].wait()
        pairs = [
            weighted_sums(lambda i: kept_ref[f, i : i + 8, c : c + 128], extent) for c in range(0, width, 128)
        ]
        for k, sums in enumerate(zip(*pairs)):
            row = jnp.concatenate(sums, axis=1)
            mx_ref[k, f : f + 1, :] = row
            total_ref[k, f : f + 1, :] = row
        head = kept_ref[f, 0:1]
        tail = kept_ref[f, extent - 1 : extent]
        mx_ref[2, f : f + 1, :] = jnp.where(even, tail, head)
        ox_ref[f : f + 1, :] = jnp.where(even, head, tail)


def first_moments(cells):
    count, extent, width = cells.shape
    shapes = (cells.shape, (3, count, width), (2, count, width), (count, width))
    return pl.pallas_call(
        first_moments_kernel,
        in_specs=[pl.BlockSpec(memory_space=pl.ANY)],
        out_specs=[pl.BlockSpec(memory_space=pltpu.VMEM)] * 4,
        out_shape=[jax.ShapeDtypeStruct(shape, jnp.float32) for shape in shapes],
        scratch_shapes=[pltpu.SemaphoreType.DMA((count,))],
        compiler_params=pltpu.CompilerParams(vmem_limit_bytes=VMEM_FULL),
        cost_estimate=COST_SMALL,
        name="moments_first",
    )(cells)


def second_moments_kernel(u_ref, after_ref, wx_ref, wy_ref, my_ref, oy_ref, rows_ref):
    even = lax.axis_index("gy") % 2 == 0
    rows_ref[0:1] = wx_ref[pl.ds(lax.axis_index("gx"), 1), :]
    rows_ref[1:2] = wy_ref[pl.ds(lax.axis_index("gy"), 1), :]
    count, extent, width = u_ref.shape
    half = width // 2
    whole = ROOT**half
    for f in range(count):
        turned = [u_ref[f, :, c : c + 128].T for c in range(0, width, 128)]
        sums = []
        for part in range(2):
            piece = lambda i: turned[(part * half + i) // 128][i % 128 : i % 128 + 8]
            sums.extend(weighted_sums(piece, half))
        low, high = turned[0][0:1], turned[-1][127:128]
        rows = [
            sums[2] + whole * sums[0],
            sums[1] + whole * sums[3],
            jnp.where(even, high, low),
        ]
        for k, row in enumerate(rows):
            my_ref[k, f : f + 1, :] = row
        rows = [
            jnp.where(even, low, high),
            sums[0],
            sums[3],
            turned[half // 128 - 1][127:128],
            turned[half // 128][0:1],
        ]
        for k, row in enumerate(rows):
            oy_ref[k, f : f + 1, :] = row


def second_moments(cells, after, table_x, table_y):
    count, extent, width = cells.shape
    return pl.pallas_call(
        second_moments_kernel,
        in_specs=[
            pl.BlockSpec(memory_space=pltpu.VMEM),
            pl.BlockSpec(memory_space=pl.ANY),
            pl.BlockSpec(memory_space=pltpu.VMEM),
            pl.BlockSpec(memory_space=pltpu.VMEM),
        ],
        out_specs=[pl.BlockSpec(memory_space=pltpu.VMEM)] * 3,
        out_shape=[
            jax.ShapeDtypeStruct(shape, jnp.float32) for shape in ((3, count, extent), (5, count, extent), (2, 128))
        ],
        compiler_params=pltpu.CompilerParams(vmem_limit_bytes=VMEM),
        cost_estimate=COST_SMALL,
        name="moments_second",
    )(cells, after, jnp.asarray(table_x), jnp.asarray(table_y))


def first_kernel(u_ref, v_ref, far_ref, near_ref, metric_ref, h_ref, c_ref, out_ref, one_ref, two_ref, done_ref, sems):
    even = lax.axis_index("gx") % 2 == 0
    count, extent, width = u_ref.shape
    row = lax.broadcasted_iota(jnp.int32, (extent, extent), 0)
    column = lax.broadcasted_iota(jnp.int32, (extent, extent), 1)
    metric = jnp.sum(jnp.where(row == column, metric_ref[...], 0.0), axis=1, keepdims=True)
    high, low = split(h_ref[...] * metric)
    one_ref[:, :extent] = high
    one_ref[:, extent:] = high
    two_ref[:, :extent] = low
    scaled = c_ref[...] * metric
    c_high = scaled.astype(jnp.bfloat16).astype(jnp.float32)
    lane = lax.broadcasted_iota(jnp.int32, scaled.shape, 1)
    two_ref[:, extent:] = jnp.where(lane < 16, c_high, scaled - c_high).astype(jnp.bfloat16)
    blank = jnp.zeros((4, width), jnp.float32)
    copies = []
    for f in range(count):
        high, low = split(u_ref[f])
        far, near = far_ref[f : f + 1, :], near_ref[2, f : f + 1, :]
        edges = [jnp.where(even, far, near), jnp.where(even, near, far)]
        rows = jnp.concatenate([v_ref[k, f : f + 1, :] for k in range(2)] + edges + [blank], axis=0)
        total = dot(one_ref[...], jnp.concatenate([high, low], axis=0))
        done_ref[f] = total + dot(two_ref[...], jnp.concatenate([high, stacked(rows)], axis=0))
        copies.append(pltpu.make_async_copy(done_ref.at[f], out_ref.at[f], sems.at[f]))
        copies[-1].start()
    for copy in copies:
        copy.wait()


def first(cells, outside, far, near, metric):
    count, extent, width = cells.shape
    h = kernel_matrix(extent).astype(np.float32)
    c = np.zeros((extent, 32), np.float64)
    columns = border_columns(extent)
    for k in range(3):
        c[:, 8 * k : 8 * k + 4] = columns.T
    return pl.pallas_call(
        first_kernel,
        in_specs=[pl.BlockSpec(memory_space=pltpu.VMEM)] * 7,
        out_specs=pl.BlockSpec(memory_space=pl.ANY),
        out_shape=jax.ShapeDtypeStruct(cells.shape, jnp.float32),
        scratch_shapes=[
            pltpu.VMEM((extent, 2 * extent), jnp.bfloat16),
            pltpu.VMEM((extent, extent + 32), jnp.bfloat16),
            pltpu.VMEM(cells.shape, jnp.float32),
            pltpu.SemaphoreType.DMA((count,)),
        ],
        compiler_params=pltpu.CompilerParams(vmem_limit_bytes=VMEM),
        cost_estimate=COST_FIRST,
        name="slope_first",
    )(cells, outside, far, near, metric.reshape(1, extent), jnp.asarray(h), jnp.asarray(c.astype(np.float32)))


def second_kernel(
    u_ref, outside_ref, own_ref, near_ref, three_ref, seven_ref, metric_ref, h_ref, c_ref, out_ref, done_ref, sems
):
    index = lax.axis_index("gy")
    even = index % 2 == 0
    third = (index + index // 2) % 2 == 1
    count, extent, width = u_ref.shape
    half = width // 2
    ratio = ROOT**half
    copies = []
    for f in range(count):
        left, right = outside_ref[0, f : f + 1, :], outside_ref[1, f : f + 1, :]
        near = near_ref[2, f : f + 1, :]
        far = jnp.where(third, three_ref[2, f : f + 1, :], seven_ref[2, f : f + 1, :])
        rows = stacked(
            jnp.concatenate(
                [
                    left,
                    own_ref[2, f : f + 1, :] + ratio * right,
                    jnp.where(even, far, near),
                    own_ref[4, f : f + 1, :],
                    own_ref[1, f : f + 1, :] + ratio * left,
                    right,
                    own_ref[3, f : f + 1, :],
                    jnp.where(even, near, far),
                ],
                axis=0,
            )
        )
        for part in range(2):
            at = slice(part * half, (part + 1) * half)
            high, low = split(u_ref[f, :, at])
            total = dot(high, h_ref[0]) + dot(low, h_ref[0]) + dot(high, h_ref[1])
            total = total + lax.dot_general(
                rows, c_ref[:, at], (((0,), (0,)), ((), ())), preferred_element_type=jnp.float32
            )
            done_ref[f, :, at] = total * metric_ref[:, at]
        copies.append(pltpu.make_async_copy(done_ref.at[f], out_ref.at[f], sems.at[f]))
        copies[-1].start()
    for copy in copies:
        copy.wait()


def halves(value):
    high = value.astype(np.float32).astype(jnp.bfloat16)
    return high, (value - high.astype(np.float64)).astype(np.float32).astype(jnp.bfloat16)


def second(cells, outside, own, replies, metric):
    count, extent, width = cells.shape
    half = width // 2
    h = np.stack(halves(kernel_matrix(half).T))
    c = np.zeros((8, width), np.float64)
    c[:4, :half] = border_columns(half)
    c[4:, half:] = border_columns(half)
    high, low = halves(c)
    c = np.concatenate([high, high, low, np.zeros_like(high)])
    return pl.pallas_call(
        second_kernel,
        in_specs=[pl.BlockSpec(memory_space=pltpu.VMEM)] * 9,
        out_specs=pl.BlockSpec(memory_space=pl.ANY),
        out_shape=jax.ShapeDtypeStruct(cells.shape, jnp.float32),
        scratch_shapes=[pltpu.VMEM(cells.shape, jnp.float32), pltpu.SemaphoreType.DMA((count,))],
        compiler_params=pltpu.CompilerParams(vmem_limit_bytes=VMEM_SECOND),
        cost_estimate=COST_SECOND,
        name="slope_second",
    )(cells, outside, own, *replies, metric.reshape(1, width), jnp.asarray(h), jnp.asarray(c))


def scan_table(devices, extent, masks):
    ratio = ROOT**extent
    table = np.zeros((devices, 128), np.float64)
    for d in range(devices):
        row = []
        base = 1
        for level in masks:
            size = len(level) + 1
            mine = d // base % size
            place = d % base
            row += [ratio ** (base * (size - 1 - mine)), ratio ** (base * mine)]
            for other in range(1, size):
                theirs = mine ^ other
                row += [ratio ** (base * (size - 1 - theirs)), ratio ** (base * theirs)]
                if theirs < mine:
                    row += [ratio ** (base * (mine - theirs - 1) + place), 0.0]
                else:
                    row += [0.0, ratio ** (base * (theirs - mine) - 1 - place)]
            base *= size
        row += [ratio**d / (1.0 - ratio**devices), ratio ** (devices - 1 - d) / (1.0 - ratio**devices)]
        table[d, : len(row)] = row
    return table.astype(np.float32)


def swap(block, axis, mask):
    return lax.ppermute(block, axis, [(i, i ^ mask) for i in range(lax.axis_size(axis))])


def swap_odd(block, axis):
    count = lax.axis_size(axis)
    return lax.ppermute(block, axis, [(i, (i + (1 if i % 2 else -1)) % count) for i in range(count)])


def after(value, *others):
    return lax.optimization_barrier((value, *others))[0]


def scan_round(row, at, total, outside, replies):
    pair = lambda k: row[k : k + 2][:, None, None]
    grown = pair(at) * total
    at += 2
    for reply in replies:
        grown = grown + pair(at) * reply
        term = pair(at + 2) * reply
        outside = term if outside is None else outside + term
        at += 4
    return at, grown, outside


def shards(fields, metric_first, metric_second):
    fields_count, planes, extent, width = fields.shape
    cells = fields.reshape(fields_count * planes, extent, width)
    cells, message_x, total_x, spare_x = first_moments(cells)
    far_x = swap_odd(spare_x, "gx")
    tables = (
        scan_table(lax.axis_size("gx"), extent, MASKS_X),
        scan_table(lax.axis_size("gy"), width, MASKS_Y),
    )
    message_y, own_y, rows = second_moments(cells, spare_x, *tables)
    message_y = after(message_y, far_x)
    at_x, outside_x = 0, None
    at_y, outside_y, total_y, replies_y = 0, None, message_y[:2], []
    for number, (level_x, level_y) in enumerate(zip(MASKS_X, MASKS_Y)):
        replies = [swap(message_x if number == 0 and mask == 1 else total_x, "gx", mask) for mask in level_x]
        if number == 0:
            near_x = replies[0]
            message = message_y
        else:
            message = after(jnp.concatenate([total_y, own_y[:1]]), total_x)
        (reply,) = [swap(message, "gy", mask) for mask in level_y]
        replies_y.append(reply)
        at_x, total_x, outside_x = scan_round(rows[0], at_x, total_x, outside_x, [r[:2] for r in replies])
        at_y, total_y, outside_y = scan_round(rows[1], at_y, total_y, outside_y, [reply[:2]])
    outside_x = outside_x + rows[0, at_x : at_x + 2][:, None, None] * total_x
    outside_y = outside_y + rows[1, at_y : at_y + 2][:, None, None] * total_y
    slope_second = second(cells, outside_y, own_y, replies_y, metric_second)
    slope_first = first(cells, outside_x, far_x, near_x, metric_first)
    return slope_first.reshape(fields.shape), slope_second.reshape(fields.shape)


def solution(mesh):
    return jax.shard_map(
        shards,
        mesh=mesh,
        in_specs=(P(None, None, "gx", "gy"), P("gx"), P("gy")),
        out_specs=(P(None, None, "gx", "gy"), P(None, None, "gx", "gy")),
        check_vma=False,
    )
```

```python
import functools
import math
import numpy as np
import jax
import jax.numpy as jnp
from jax import lax
from jax.experimental import pallas as pl
from jax.experimental.pallas import tpu as pltpu
from jax.sharding import PartitionSpec as P

ALPHA = 0.47
STENCIL_NEAR = (ALPHA + 2.0) / 3.0
STENCIL_FAR = (4.0 * ALPHA - 1.0) / 12.0
ROOT = (math.sqrt(1.0 - 4.0 * ALPHA * ALPHA) - 1.0) / (2.0 * ALPHA)
PEAK = 1.0 / math.sqrt(1.0 - 4.0 * ALPHA * ALPHA)
DECAY = PEAK * (STENCIL_NEAR * (ROOT - 1.0 / ROOT) + STENCIL_FAR * (ROOT**2 - ROOT**-2))
NEXT = PEAK * STENCIL_FAR * (1.0 / ROOT - ROOT)
MASKS_X = ((1, 2, 3), (7,), (8, 16, 24))
MASKS_Y = ((1,), (3,), (7,))
VMEM = 16 * 1024 * 1024
VMEM_FULL = 50 * 1024 * 1024
VMEM_SECOND = 16 * 1024 * 1024
COST_SMALL = pl.CostEstimate(flops=8_000_000, bytes_accessed=8_000_000, transcendentals=0)
COST_FIRST = pl.CostEstimate(flops=3_000_000_000, bytes_accessed=8_000_000, transcendentals=0)
COST_SECOND = pl.CostEstimate(flops=300_000_000, bytes_accessed=8_000_000, transcendentals=0)


def kernel_matrix(extent):
    gap = np.arange(extent)[:, None] - np.arange(extent)[None, :]
    size = np.abs(gap)
    value = DECAY * ROOT ** size.astype(np.float64) + NEXT * (size == 1)
    return np.sign(gap) * value


def border_columns(extent):
    place = np.arange(extent)
    left = DECAY * ROOT ** place.astype(np.float64)
    return np.stack([left, -left[::-1], NEXT * (place == 0), -NEXT * (place == extent - 1)])


def split(value):
    high = value.astype(jnp.bfloat16)
    return high, (value - high.astype(jnp.float32)).astype(jnp.bfloat16)


def dot(left, right):
    return jnp.dot(left, right, preferred_element_type=jnp.float32)


def stacked(rows):
    high = rows.astype(jnp.bfloat16).astype(jnp.float32)
    low = (rows - high).astype(jnp.bfloat16).astype(jnp.float32)
    return jnp.concatenate([high, low, high, jnp.zeros_like(high)], axis=0).astype(jnp.bfloat16)


def row_weights(rows):
    place = lax.broadcasted_iota(jnp.int32, (8, 128), 0)
    down = jnp.zeros((8, 128), jnp.float32)
    up = jnp.zeros((8, 128), jnp.float32)
    for s in range(8):
        down = jnp.where(place == s, ROOT ** (8 - s), down)
        up = jnp.where(place == s, ROOT ** (s + 1), up)
    return down, up


def weighted_sums(load, extent):
    down, up = row_weights(8)
    right = left = None
    for i in range(0, extent, 8):
        rows = load(i)
        right = rows if right is None else right * ROOT**8 + rows
        rows = load(extent - 8 - i)
        left = rows if left is None else left * ROOT**8 + rows
    return jnp.sum(right * down, axis=0, keepdims=True), jnp.sum(left * up, axis=0, keepdims=True)


def first_moments_kernel(u_ref, kept_ref, mx_ref, total_ref, ox_ref, sems):
    even = lax.axis_index("gx") % 2 == 0
    count, extent, width = u_ref.shape
    copies = [pltpu.make_async_copy(u_ref.at[f], kept_ref.at[f], sems.at[f]) for f in range(count)]
    for copy in copies:
        copy.start()
    for f in range(count):
        copies[f].wait()
        pairs = [
            weighted_sums(lambda i: kept_ref[f, i : i + 8, c : c + 128], extent) for c in range(0, width, 128)
        ]
        for k, sums in enumerate(zip(*pairs)):
            row = jnp.concatenate(sums, axis=1)
            mx_ref[k, f : f + 1, :] = row
            total_ref[k, f : f + 1, :] = row
        head = kept_ref[f, 0:1]
        tail = kept_ref[f, extent - 1 : extent]
        mx_ref[2, f : f + 1, :] = jnp.where(even, tail, head)
        ox_ref[f : f + 1, :] = jnp.where(even, head, tail)


def first_moments(cells):
    count, extent, width = cells.shape
    shapes = (cells.shape, (3, count, width), (2, count, width), (count, width))
    return pl.pallas_call(
        first_moments_kernel,
        in_specs=[pl.BlockSpec(memory_space=pl.ANY)],
        out_specs=[pl.BlockSpec(memory_space=pltpu.VMEM)] * 4,
        out_shape=[jax.ShapeDtypeStruct(shape, jnp.float32) for shape in shapes],
        scratch_shapes=[pltpu.SemaphoreType.DMA((count,))],
        compiler_params=pltpu.CompilerParams(vmem_limit_bytes=VMEM_FULL),
        cost_estimate=COST_SMALL,
        name="moments_first",
    )(cells)


def second_moments_kernel(u_ref, after_ref, wx_ref, wy_ref, my_ref, oy_ref, rows_ref):
    even = lax.axis_index("gy") % 2 == 0
    rows_ref[0:1] = wx_ref[pl.ds(lax.axis_index("gx"), 1), :]
    rows_ref[1:2] = wy_ref[pl.ds(lax.axis_index("gy"), 1), :]
    count, extent, width = u_ref.shape
    half = width // 2
    whole = ROOT**half
    for f in range(count):
        turned = [u_ref[f, :, c : c + 128].T for c in range(0, width, 128)]
        sums = []
        for part in range(2):
            piece = lambda i: turned[(part * half + i) // 128][i % 128 : i % 128 + 8]
            sums.extend(weighted_sums(piece, half))
        low, high = turned[0][0:1], turned[-1][127:128]
        rows = [
            sums[2] + whole * sums[0],
            sums[1] + whole * sums[3],
            jnp.where(even, high, low),
        ]
        for k, row in enumerate(rows):
            my_ref[k, f : f + 1, :] = row
        rows = [
            jnp.where(even, low, high),
            sums[0],
            sums[3],
            turned[half // 128 - 1][127:128],
            turned[half // 128][0:1],
        ]
        for k, row in enumerate(rows):
            oy_ref[k, f : f + 1, :] = row


def second_moments(cells, after, table_x, table_y):
    count, extent, width = cells.shape
    return pl.pallas_call(
        second_moments_kernel,
        in_specs=[
            pl.BlockSpec(memory_space=pltpu.VMEM),
            pl.BlockSpec(memory_space=pl.ANY),
            pl.BlockSpec(memory_space=pltpu.VMEM),
            pl.BlockSpec(memory_space=pltpu.VMEM),
        ],
        out_specs=[pl.BlockSpec(memory_space=pltpu.VMEM)] * 3,
        out_shape=[
            jax.ShapeDtypeStruct(shape, jnp.float32) for shape in ((3, count, extent), (5, count, extent), (2, 128))
        ],
        compiler_params=pltpu.CompilerParams(vmem_limit_bytes=VMEM),
        cost_estimate=COST_SMALL,
        name="moments_second",
    )(cells, after, jnp.asarray(table_x), jnp.asarray(table_y))


def first_kernel(u_ref, v_ref, far_ref, near_ref, metric_ref, h_ref, c_ref, out_ref, one_ref, two_ref, done_ref, sems):
    even = lax.axis_index("gx") % 2 == 0
    count, extent, width = u_ref.shape
    row = lax.broadcasted_iota(jnp.int32, (extent, extent), 0)
    column = lax.broadcasted_iota(jnp.int32, (extent, extent), 1)
    metric = jnp.sum(jnp.where(row == column, metric_ref[...], 0.0), axis=1, keepdims=True)
    high, low = split(h_ref[...] * metric)
    one_ref[:, :extent] = high
    one_ref[:, extent:] = high
    two_ref[:, :extent] = low
    scaled = c_ref[...] * metric
    c_high = scaled.astype(jnp.bfloat16).astype(jnp.float32)
    lane = lax.broadcasted_iota(jnp.int32, scaled.shape, 1)
    two_ref[:, extent:] = jnp.where(lane < 16, c_high, scaled - c_high).astype(jnp.bfloat16)
    blank = jnp.zeros((4, width), jnp.float32)
    copies = []
    for f in range(count):
        high, low = split(u_ref[f])
        far, near = far_ref[f : f + 1, :], near_ref[2, f : f + 1, :]
        edges = [jnp.where(even, far, near), jnp.where(even, near, far)]
        rows = jnp.concatenate([v_ref[k, f : f + 1, :] for k in range(2)] + edges + [blank], axis=0)
        total = dot(one_ref[...], jnp.concatenate([high, low], axis=0))
        done_ref[f] = total + dot(two_ref[...], jnp.concatenate([high, stacked(rows)], axis=0))
        copies.append(pltpu.make_async_copy(done_ref.at[f], out_ref.at[f], sems.at[f]))
        copies[-1].start()
    for copy in copies:
        copy.wait()


def first(cells, outside, far, near, metric):
    count, extent, width = cells.shape
    h = kernel_matrix(extent).astype(np.float32)
    c = np.zeros((extent, 32), np.float64)
    columns = border_columns(extent)
    for k in range(3):
        c[:, 8 * k : 8 * k + 4] = columns.T
    return pl.pallas_call(
        first_kernel,
        in_specs=[pl.BlockSpec(memory_space=pltpu.VMEM)] * 7,
        out_specs=pl.BlockSpec(memory_space=pl.ANY),
        out_shape=jax.ShapeDtypeStruct(cells.shape, jnp.float32),
        scratch_shapes=[
            pltpu.VMEM((extent, 2 * extent), jnp.bfloat16),
            pltpu.VMEM((extent, extent + 32), jnp.bfloat16),
            pltpu.VMEM(cells.shape, jnp.float32),
            pltpu.SemaphoreType.DMA((count,)),
        ],
        compiler_params=pltpu.CompilerParams(vmem_limit_bytes=VMEM),
        cost_estimate=COST_FIRST,
        name="slope_first",
    )(cells, outside, far, near, metric.reshape(1, extent), jnp.asarray(h), jnp.asarray(c.astype(np.float32)))


def second_kernel(
    u_ref, outside_ref, own_ref, near_ref, three_ref, seven_ref, metric_ref, h_ref, c_ref, out_ref, done_ref, sems
):
    index = lax.axis_index("gy")
    even = index % 2 == 0
    third = (index + index // 2) % 2 == 1
    count, extent, width = u_ref.shape
    half = width // 2
    ratio = ROOT**half
    copies = []
    for f in range(count):
        left, right = outside_ref[0, f : f + 1, :], outside_ref[1, f : f + 1, :]
        near = near_ref[2, f : f + 1, :]
        far = jnp.where(third, three_ref[2, f : f + 1, :], seven_ref[2, f : f + 1, :])
        rows = stacked(
            jnp.concatenate(
                [
                    left,
                    own_ref[2, f : f + 1, :] + ratio * right,
                    jnp.where(even, far, near),
                    own_ref[4, f : f + 1, :],
                    own_ref[1, f : f + 1, :] + ratio * left,
                    right,
                    own_ref[3, f : f + 1, :],
                    jnp.where(even, near, far),
                ],
                axis=0,
            )
        )
        for part in range(2):
            at = slice(part * half, (part + 1) * half)
            high, low = split(u_ref[f, :, at])
            total = dot(high, h_ref[0]) + dot(low, h_ref[0]) + dot(high, h_ref[1])
            total = total + lax.dot_general(
                rows, c_ref[:, at], (((0,), (0,)), ((), ())), preferred_element_type=jnp.float32
            )
            done_ref[f, :, at] = total * metric_ref[:, at]
        copies.append(pltpu.make_async_copy(done_ref.at[f], out_ref.at[f], sems.at[f]))
        copies[-1].start()
    for copy in copies:
        copy.wait()


def halves(value):
    high = value.astype(np.float32).astype(jnp.bfloat16)
    return high, (value - high.astype(np.float64)).astype(np.float32).astype(jnp.bfloat16)


def second(cells, outside, own, replies, metric):
    count, extent, width = cells.shape
    half = width // 2
    h = np.stack(halves(kernel_matrix(half).T))
    c = np.zeros((8, width), np.float64)
    c[:4, :half] = border_columns(half)
    c[4:, half:] = border_columns(half)
    high, low = halves(c)
    c = np.concatenate([high, high, low, np.zeros_like(high)])
    return pl.pallas_call(
        second_kernel,
        in_specs=[pl.BlockSpec(memory_space=pltpu.VMEM)] * 9,
        out_specs=pl.BlockSpec(memory_space=pl.ANY),
        out_shape=jax.ShapeDtypeStruct(cells.shape, jnp.float32),
        scratch_shapes=[pltpu.VMEM(cells.shape, jnp.float32), pltpu.SemaphoreType.DMA((count,))],
        compiler_params=pltpu.CompilerParams(vmem_limit_bytes=VMEM_SECOND),
        cost_estimate=COST_SECOND,
        name="slope_second",
    )(cells, outside, own, *replies, metric.reshape(1, width), jnp.asarray(h), jnp.asarray(c))


def scan_table(devices, extent, masks):
    ratio = ROOT**extent
    table = np.zeros((devices, 128), np.float64)
    for d in range(devices):
        row = []
        base = 1
        for level in masks:
            size = len(level) + 1
            mine = d // base % size
            place = d % base
            row += [ratio ** (base * (size - 1 - mine)), ratio ** (base * mine)]
            for other in range(1, size):
                theirs = mine ^ other
                row += [ratio ** (base * (size - 1 - theirs)), ratio ** (base * theirs)]
                if theirs < mine:
                    row += [ratio ** (base * (mine - theirs - 1) + place), 0.0]
                else:
                    row += [0.0, ratio ** (base * (theirs - mine) - 1 - place)]
            base *= size
        row += [ratio**d / (1.0 - ratio**devices), ratio ** (devices - 1 - d) / (1.0 - ratio**devices)]
        table[d, : len(row)] = row
    return table.astype(np.float32)


def swap(block, axis, mask):
    return lax.ppermute(block, axis, [(i, i ^ mask) for i in range(lax.axis_size(axis))])


def swap_odd(block, axis):
    count = lax.axis_size(axis)
    return lax.ppermute(block, axis, [(i, (i + (1 if i % 2 else -1)) % count) for i in range(count)])


def after(value, *others):
    return lax.optimization_barrier((value, *others))[0]


def scan_round(row, at, total, outside, replies):
    pair = lambda k: row[k : k + 2][:, None, None]
    grown = pair(at) * total
    at += 2
    for reply in replies:
        grown = grown + pair(at) * reply
        term = pair(at + 2) * reply
        outside = term if outside is None else outside + term
        at += 4
    return at, grown, outside


def shards(fields, metric_first, metric_second):
    fields_count, planes, extent, width = fields.shape
    cells = fields.reshape(fields_count * planes, extent, width)
    cells, message_x, total_x, spare_x = first_moments(cells)
    far_x = swap_odd(spare_x, "gx")
    tables = (
        scan_table(lax.axis_size("gx"), extent, MASKS_X),
        scan_table(lax.axis_size("gy"), width, MASKS_Y),
    )
    message_y, own_y, rows = second_moments(cells, spare_x, *tables)
    message_y = after(message_y, far_x)
    at_x, outside_x = 0, None
    at_y, outside_y, total_y, replies_y = 0, None, message_y[:2], []
    for number, (level_x, level_y) in enumerate(zip(MASKS_X, MASKS_Y)):
        replies = [swap(message_x if number == 0 and mask == 1 else total_x, "gx", mask) for mask in level_x]
        if number == 0:
            near_x = replies[0]
            message = message_y
        else:
            message = after(jnp.concatenate([total_y, own_y[:1]]), total_x)
        (reply,) = [swap(message, "gy", mask) for mask in level_y]
        replies_y.append(reply)
        at_x, total_x, outside_x = scan_round(rows[0], at_x, total_x, outside_x, [r[:2] for r in replies])
        if number == 1:
            reply = after(reply, total_x)
            replies_y[-1] = reply
        at_y, total_y, outside_y = scan_round(rows[1], at_y, total_y, outside_y, [reply[:2]])
    outside_x = outside_x + rows[0, at_x : at_x + 2][:, None, None] * total_x
    outside_y = outside_y + rows[1, at_y : at_y + 2][:, None, None] * total_y
    slope_second = second(cells, outside_y, own_y, replies_y, metric_second)
    slope_first = first(cells, outside_x, far_x, near_x, metric_first)
    return slope_first.reshape(fields.shape), slope_second.reshape(fields.shape)


def solution(mesh):
    return jax.shard_map(
        shards,
        mesh=mesh,
        in_specs=(P(None, None, "gx", "gy"), P("gx"), P("gy")),
        out_specs=(P(None, None, "gx", "gy"), P(None, None, "gx", "gy")),
        check_vma=False,
    )
```

```python
import functools
import math
import numpy as np
import jax
import jax.numpy as jnp
from jax import lax
from jax.experimental import pallas as pl
from jax.experimental.pallas import tpu as pltpu
from jax.sharding import PartitionSpec as P

ALPHA = 0.47
STENCIL_NEAR = (ALPHA + 2.0) / 3.0
STENCIL_FAR = (4.0 * ALPHA - 1.0) / 12.0
ROOT = (math.sqrt(1.0 - 4.0 * ALPHA * ALPHA) - 1.0) / (2.0 * ALPHA)
PEAK = 1.0 / math.sqrt(1.0 - 4.0 * ALPHA * ALPHA)
DECAY = PEAK * (STENCIL_NEAR * (ROOT - 1.0 / ROOT) + STENCIL_FAR * (ROOT**2 - ROOT**-2))
NEXT = PEAK * STENCIL_FAR * (1.0 / ROOT - ROOT)
MASKS_X = ((1, 2, 3), (7,), (8, 16, 24))
MASKS_Y = ((1,), (3,), (7,))
VMEM = 16 * 1024 * 1024
VMEM_FULL = 50 * 1024 * 1024
VMEM_SECOND = 16 * 1024 * 1024
COST_SMALL = pl.CostEstimate(flops=8_000_000, bytes_accessed=8_000_000, transcendentals=0)
COST_FIRST = pl.CostEstimate(flops=3_000_000_000, bytes_accessed=8_000_000, transcendentals=0)
COST_SECOND = pl.CostEstimate(flops=300_000_000, bytes_accessed=8_000_000, transcendentals=0)


def kernel_matrix(extent):
    gap = np.arange(extent)[:, None] - np.arange(extent)[None, :]
    size = np.abs(gap)
    value = DECAY * ROOT ** size.astype(np.float64) + NEXT * (size == 1)
    return np.sign(gap) * value


def border_columns(extent):
    place = np.arange(extent)
    left = DECAY * ROOT ** place.astype(np.float64)
    return np.stack([left, -left[::-1], NEXT * (place == 0), -NEXT * (place == extent - 1)])


def split(value):
    high = value.astype(jnp.bfloat16)
    return high, (value - high.astype(jnp.float32)).astype(jnp.bfloat16)


def dot(left, right):
    return jnp.dot(left, right, preferred_element_type=jnp.float32)


def stacked(rows):
    high = rows.astype(jnp.bfloat16).astype(jnp.float32)
    low = (rows - high).astype(jnp.bfloat16).astype(jnp.float32)
    return jnp.concatenate([high, low, high, jnp.zeros_like(high)], axis=0).astype(jnp.bfloat16)


def row_weights(rows):
    place = lax.broadcasted_iota(jnp.int32, (8, 128), 0)
    down = jnp.zeros((8, 128), jnp.float32)
    up = jnp.zeros((8, 128), jnp.float32)
    for s in range(8):
        down = jnp.where(place == s, ROOT ** (8 - s), down)
        up = jnp.where(place == s, ROOT ** (s + 1), up)
    return down, up


def weighted_sums(load, extent):
    down, up = row_weights(8)
    right = left = None
    for i in range(0, extent, 8):
        rows = load(i)
        right = rows if right is None else right * ROOT**8 + rows
        rows = load(extent - 8 - i)
        left = rows if left is None else left * ROOT**8 + rows
    return jnp.sum(right * down, axis=0, keepdims=True), jnp.sum(left * up, axis=0, keepdims=True)


def first_moments_kernel(u_ref, kept_ref, mx_ref, total_ref, ox_ref, sems):
    even = lax.axis_index("gx") % 2 == 0
    count, extent, width = u_ref.shape
    copies = [pltpu.make_async_copy(u_ref.at[f], kept_ref.at[f], sems.at[f]) for f in range(count)]
    for copy in copies:
        copy.start()
    for f in range(count):
        copies[f].wait()
        pairs = [
            weighted_sums(lambda i: kept_ref[f, i : i + 8, c : c + 128], extent) for c in range(0, width, 128)
        ]
        for k, sums in enumerate(zip(*pairs)):
            row = jnp.concatenate(sums, axis=1)
            mx_ref[k, f : f + 1, :] = row
            total_ref[k, f : f + 1, :] = row
        head = kept_ref[f, 0:1]
        tail = kept_ref[f, extent - 1 : extent]
        mx_ref[2, f : f + 1, :] = jnp.where(even, tail, head)
        ox_ref[f : f + 1, :] = jnp.where(even, head, tail)


def first_moments(cells):
    count, extent, width = cells.shape
    shapes = (cells.shape, (3, count, width), (2, count, width), (count, width))
    return pl.pallas_call(
        first_moments_kernel,
        in_specs=[pl.BlockSpec(memory_space=pl.ANY)],
        out_specs=[pl.BlockSpec(memory_space=pltpu.VMEM)] * 4,
        out_shape=[jax.ShapeDtypeStruct(shape, jnp.float32) for shape in shapes],
        scratch_shapes=[pltpu.SemaphoreType.DMA((count,))],
        compiler_params=pltpu.CompilerParams(vmem_limit_bytes=VMEM_FULL),
        cost_estimate=COST_SMALL,
        name="moments_first",
    )(cells)


def second_moments_kernel(u_ref, after_ref, wx_ref, wy_ref, my_ref, oy_ref, rows_ref):
    even = lax.axis_index("gy") % 2 == 0
    rows_ref[0:1] = wx_ref[pl.ds(lax.axis_index("gx"), 1), :]
    rows_ref[1:2] = wy_ref[pl.ds(lax.axis_index("gy"), 1), :]
    count, extent, width = u_ref.shape
    half = width // 2
    whole = ROOT**half
    for f in range(count):
        turned = [u_ref[f, :, c : c + 128].T for c in range(0, width, 128)]
        sums = []
        for part in range(2):
            piece = lambda i: turned[(part * half + i) // 128][i % 128 : i % 128 + 8]
            sums.extend(weighted_sums(piece, half))
        low, high = turned[0][0:1], turned[-1][127:128]
        rows = [
            sums[2] + whole * sums[0],
            sums[1] + whole * sums[3],
            jnp.where(even, high, low),
        ]
        for k, row in enumerate(rows):
            my_ref[k, f : f + 1, :] = row
        rows = [
            jnp.where(even, low, high),
            sums[0],
            sums[3],
            turned[half // 128 - 1][127:128],
            turned[half // 128][0:1],
        ]
        for k, row in enumerate(rows):
            oy_ref[k, f : f + 1, :] = row


def second_moments(cells, after, table_x, table_y):
    count, extent, width = cells.shape
    return pl.pallas_call(
        second_moments_kernel,
        in_specs=[
            pl.BlockSpec(memory_space=pltpu.VMEM),
            pl.BlockSpec(memory_space=pl.ANY),
            pl.BlockSpec(memory_space=pltpu.VMEM),
            pl.BlockSpec(memory_space=pltpu.VMEM),
        ],
        out_specs=[pl.BlockSpec(memory_space=pltpu.VMEM)] * 3,
        out_shape=[
            jax.ShapeDtypeStruct(shape, jnp.float32) for shape in ((3, count, extent), (5, count, extent), (2, 128))
        ],
        compiler_params=pltpu.CompilerParams(vmem_limit_bytes=VMEM),
        cost_estimate=COST_SMALL,
        name="moments_second",
    )(cells, after, jnp.asarray(table_x), jnp.asarray(table_y))


def first_kernel(u_ref, v_ref, far_ref, near_ref, metric_ref, h_ref, c_ref, out_ref, one_ref, two_ref, done_ref, sems):
    even = lax.axis_index("gx") % 2 == 0
    count, extent, width = u_ref.shape
    row = lax.broadcasted_iota(jnp.int32, (extent, extent), 0)
    column = lax.broadcasted_iota(jnp.int32, (extent, extent), 1)
    metric = jnp.sum(jnp.where(row == column, metric_ref[...], 0.0), axis=1, keepdims=True)
    high, low = split(h_ref[...] * metric)
    one_ref[:, :extent] = high
    one_ref[:, extent:] = high
    two_ref[:, :extent] = low
    scaled = c_ref[...] * metric
    c_high = scaled.astype(jnp.bfloat16).astype(jnp.float32)
    lane = lax.broadcasted_iota(jnp.int32, scaled.shape, 1)
    two_ref[:, extent:] = jnp.where(lane < 16, c_high, scaled - c_high).astype(jnp.bfloat16)
    blank = jnp.zeros((4, width), jnp.float32)
    copies = []
    for f in range(count):
        high, low = split(u_ref[f])
        far, near = far_ref[f : f + 1, :], near_ref[2, f : f + 1, :]
        edges = [jnp.where(even, far, near), jnp.where(even, near, far)]
        rows = jnp.concatenate([v_ref[k, f : f + 1, :] for k in range(2)] + edges + [blank], axis=0)
        total = dot(one_ref[...], jnp.concatenate([high, low], axis=0))
        done_ref[f] = total + dot(two_ref[...], jnp.concatenate([high, stacked(rows)], axis=0))
        copies.append(pltpu.make_async_copy(done_ref.at[f], out_ref.at[f], sems.at[f]))
        copies[-1].start()
    for copy in copies:
        copy.wait()


def first(cells, outside, far, near, metric):
    count, extent, width = cells.shape
    h = kernel_matrix(extent).astype(np.float32)
    c = np.zeros((extent, 32), np.float64)
    columns = border_columns(extent)
    for k in range(3):
        c[:, 8 * k : 8 * k + 4] = columns.T
    return pl.pallas_call(
        first_kernel,
        in_specs=[pl.BlockSpec(memory_space=pltpu.VMEM)] * 7,
        out_specs=pl.BlockSpec(memory_space=pl.ANY),
        out_shape=jax.ShapeDtypeStruct(cells.shape, jnp.float32),
        scratch_shapes=[
            pltpu.VMEM((extent, 2 * extent), jnp.bfloat16),
            pltpu.VMEM((extent, extent + 32), jnp.bfloat16),
            pltpu.VMEM(cells.shape, jnp.float32),
            pltpu.SemaphoreType.DMA((count,)),
        ],
        compiler_params=pltpu.CompilerParams(vmem_limit_bytes=VMEM),
        cost_estimate=COST_FIRST,
        name="slope_first",
    )(cells, outside, far, near, metric.reshape(1, extent), jnp.asarray(h), jnp.asarray(c.astype(np.float32)))


def second_kernel(
    u_ref, outside_ref, own_ref, near_ref, three_ref, seven_ref, metric_ref, h_ref, c_ref, out_ref, done_ref, sems
):
    index = lax.axis_index("gy")
    even = index % 2 == 0
    third = (index + index // 2) % 2 == 1
    count, extent, width = u_ref.shape
    half = width // 2
    ratio = ROOT**half
    copies = []
    for f in range(count):
        left, right = outside_ref[0, f : f + 1, :], outside_ref[1, f : f + 1, :]
        near = near_ref[2, f : f + 1, :]
        far = jnp.where(third, three_ref[2, f : f + 1, :], seven_ref[2, f : f + 1, :])
        rows = stacked(
            jnp.concatenate(
                [
                    left,
                    own_ref[2, f : f + 1, :] + ratio * right,
                    jnp.where(even, far, near),
                    own_ref[4, f : f + 1, :],
                    own_ref[1, f : f + 1, :] + ratio * left,
                    right,
                    own_ref[3, f : f + 1, :],
                    jnp.where(even, near, far),
                ],
                axis=0,
            )
        )
        for part in range(2):
            at = slice(part * half, (part + 1) * half)
            high, low = split(u_ref[f, :, at])
            total = dot(high, h_ref[0]) + dot(low, h_ref[0]) + dot(high, h_ref[1])
            total = total + lax.dot_general(
                rows, c_ref[:, at], (((0,), (0,)), ((), ())), preferred_element_type=jnp.float32
            )
            done_ref[f, :, at] = total * metric_ref[:, at]
        copies.append(pltpu.make_async_copy(done_ref.at[f], out_ref.at[f], sems.at[f]))
        copies[-1].start()
    for copy in copies:
        copy.wait()


def halves(value):
    high = value.astype(np.float32).astype(jnp.bfloat16)
    return high, (value - high.astype(np.float64)).astype(np.float32).astype(jnp.bfloat16)


def second(cells, outside, own, replies, metric):
    count, extent, width = cells.shape
    half = width // 2
    h = np.stack(halves(kernel_matrix(half).T))
    c = np.zeros((8, width), np.float64)
    c[:4, :half] = border_columns(half)
    c[4:, half:] = border_columns(half)
    high, low = halves(c)
    c = np.concatenate([high, high, low, np.zeros_like(high)])
    return pl.pallas_call(
        second_kernel,
        in_specs=[pl.BlockSpec(memory_space=pltpu.VMEM)] * 9,
        out_specs=pl.BlockSpec(memory_space=pl.ANY),
        out_shape=jax.ShapeDtypeStruct(cells.shape, jnp.float32),
        scratch_shapes=[pltpu.VMEM(cells.shape, jnp.float32), pltpu.SemaphoreType.DMA((count,))],
        compiler_params=pltpu.CompilerParams(vmem_limit_bytes=VMEM_SECOND),
        cost_estimate=COST_SECOND,
        name="slope_second",
    )(cells, outside, own, *replies, metric.reshape(1, width), jnp.asarray(h), jnp.asarray(c))


def scan_table(devices, extent, masks):
    ratio = ROOT**extent
    table = np.zeros((devices, 128), np.float64)
    for d in range(devices):
        row = []
        base = 1
        for level in masks:
            size = len(level) + 1
            mine = d // base % size
            place = d % base
            row += [ratio ** (base * (size - 1 - mine)), ratio ** (base * mine)]
            for other in range(1, size):
                theirs = mine ^ other
                row += [ratio ** (base * (size - 1 - theirs)), ratio ** (base * theirs)]
                if theirs < mine:
                    row += [ratio ** (base * (mine - theirs - 1) + place), 0.0]
                else:
                    row += [0.0, ratio ** (base * (theirs - mine) - 1 - place)]
            base *= size
        row += [ratio**d / (1.0 - ratio**devices), ratio ** (devices - 1 - d) / (1.0 - ratio**devices)]
        table[d, : len(row)] = row
    return table.astype(np.float32)


def swap(block, axis, mask):
    return lax.ppermute(block, axis, [(i, i ^ mask) for i in range(lax.axis_size(axis))])


def swap_odd(block, axis):
    count = lax.axis_size(axis)
    return lax.ppermute(block, axis, [(i, (i + (1 if i % 2 else -1)) % count) for i in range(count)])


def after(value, *others):
    return lax.optimization_barrier((value, *others))[0]


def scan_round(row, at, total, outside, replies):
    pair = lambda k: row[k : k + 2][:, None, None]
    grown = pair(at) * total
    at += 2
    for reply in replies:
        grown = grown + pair(at) * reply
        term = pair(at + 2) * reply
        outside = term if outside is None else outside + term
        at += 4
    return at, grown, outside


def shards(fields, metric_first, metric_second):
    fields_count, planes, extent, width = fields.shape
    cells = fields.reshape(fields_count * planes, extent, width)
    cells, message_x, total_x, spare_x = first_moments(cells)
    far_x = swap_odd(spare_x, "gx")
    tables = (
        scan_table(lax.axis_size("gx"), extent, MASKS_X),
        scan_table(lax.axis_size("gy"), width, MASKS_Y),
    )
    message_y, own_y, rows = second_moments(cells, spare_x, *tables)
    message_y = after(message_y, far_x)
    at_x, outside_x = 0, None
    at_y, outside_y, total_y, replies_y = 0, None, message_y[:2], []
    for number, (level_x, level_y) in enumerate(zip(MASKS_X, MASKS_Y)):
        replies = [swap(message_x if number == 0 and mask == 1 else total_x, "gx", mask) for mask in level_x]
        if number == 0:
            near_x = replies[0]
            message = message_y
        else:
            message = after(jnp.concatenate([total_y, own_y[:1]]), total_x)
        (reply,) = [swap(message, "gy", mask) for mask in level_y]
        replies_y.append(reply)
        at_x, total_x, outside_x = scan_round(rows[0], at_x, total_x, outside_x, [r[:2] for r in replies])
        if number == 1:
            reply = after(reply, total_x)
            replies_y[-1] = reply
        if number == 2:
            reply = after(reply, replies[0])
            replies_y[-1] = reply
        at_y, total_y, outside_y = scan_round(rows[1], at_y, total_y, outside_y, [reply[:2]])
    outside_x = outside_x + rows[0, at_x : at_x + 2][:, None, None] * total_x
    outside_y = outside_y + rows[1, at_y : at_y + 2][:, None, None] * total_y
    slope_second = second(cells, outside_y, own_y, replies_y, metric_second)
    slope_first = first(cells, outside_x, far_x, near_x, metric_first)
    return slope_first.reshape(fields.shape), slope_second.reshape(fields.shape)


def solution(mesh):
    return jax.shard_map(
        shards,
        mesh=mesh,
        in_specs=(P(None, None, "gx", "gy"), P("gx"), P("gy")),
        out_specs=(P(None, None, "gx", "gy"), P(None, None, "gx", "gy")),
        check_vma=False,
    )
```
